128 devices in a mesh: child: 4 (over z_hi, core), col: 32 (over y, x, z_lo).
Axes of the slice: x: 4, y: 4, z: 4 (z_hi: 2, z_lo: 2; z = z_hi * 2 + z_lo), core: 2. Of those that a mesh axis runs over, the one named last changes fastest.
Arguments:
- parent_entries: float32 [16384, 16384], P('child', 'col'), as said below
- updates: float32 [4, 8192, 8192], P('child', 'col'), as said below
- block_maps: int32 [4, 64], replicated, may hold values from 0 to 127, as said below
- live_blocks: int32 [4, 64], replicated, may hold values 0 or 1
Outputs:
- factored: float32 [16384, 16384], P('child', 'col')
The draws below stay inside these ranges and needn't reach their ends.
Inputs may be any that keep to these rules, and one draw needn't show every extreme that they name: For every sibling c and block t, block_maps[c, t] // 4 == t // 2, and each sibling's row is strictly increasing: a sibling covers two of every four aligned parent blocks, and half of the parent's blocks in all. `parent_entries`: Symmetric, with diagonal entries between 1 and 2; the assembled parent is positive definite. `updates`: each sibling's matrix is symmetric.
All inputs are finite; a program needn't handle non-finite values.
Results may differ from the reference program's by a relative error of at most 0.0001.
Values sent between devices are 32-bit elements; how exact they have to be, the bound alone decides.
A program may use at most 192 MiB of HBM per device.

```python
import jax
import jax.numpy as jnp
import numpy as np
from jax import lax

BLOCK = 128
NB = 512
PANELS = 2
SIBLINGS = 4
PARENT = 16384
CHILD = 8192


def draw_parent_entries(key, part):
    key = jax.random.fold_in(key, 11)
    first_key, second_key = jax.random.split(key)
    matrix_order = PARENT
    sample = jnp.clip(jax.random.normal(first_key, (matrix_order, matrix_order), jnp.float32), -6.0, 6.0)
    offset = 0.5 / NB
    positions = jnp.arange(matrix_order)
    same_block = positions[:, None] // NB == positions[None, :] // NB
    near_scale = 0.2 / NB ** 0.5
    spread_scale = 0.1 / PARENT ** 0.5
    scale = jnp.where(same_block, near_scale, 0.0) + spread_scale
    symmetric = (sample + sample.T) * 0.70710678 * scale + offset
    diagonal = jax.random.uniform(second_key, (matrix_order,), jnp.float32, 1.0, 2.0)
    return jnp.where(positions[:, None] == positions[None, :], diagonal[:, None], symmetric)


def draw_updates(key, part):
    key = jax.random.fold_in(key, 12)
    sample = jnp.clip(jax.random.normal(key, (SIBLINGS, CHILD, CHILD), jnp.float32), -6.0, 6.0)
    scale = 0.08 / CHILD ** 0.5
    return (sample + jnp.swapaxes(sample, 1, 2)) * (0.70710678 * scale)


def draw_block_maps(key, part):
    key = jax.random.fold_in(key, 13)
    owner_count = CHILD // BLOCK // 2
    pair_ids = jax.random.randint(key, (SIBLINGS, owner_count), 0, 6)
    pair_ids = pair_ids.at[0, 0].set(2).at[0, owner_count - 1].set(2)
    first_slot = jnp.array(np.array([0, 0, 0, 1, 1, 2], np.int32))[pair_ids]
    second_slot = jnp.array(np.array([1, 2, 3, 2, 3, 3], np.int32))[pair_ids]
    owner_base = 4 * jnp.arange(owner_count, dtype=jnp.int32)[None, :]
    paired = jnp.stack([owner_base + first_slot, owner_base + second_slot], axis=2)
    return paired.reshape(SIBLINGS, 2 * owner_count).astype(jnp.int32)


def plant(values, stream_key, smallest, high):
    longest = values.shape.index(max(values.shape))
    spots = []
    for shift in (0, 1):
        where = [jax.random.randint(jax.random.fold_in(stream_key, axis), (), 0, length) for axis, length in enumerate(values.shape)]
        where[longest] = (where[longest] + shift) % values.shape[longest]
        spots.append(tuple(where))
    return values.at[spots[0]].set(smallest).at[spots[1]].set(high)


def setup_inputs(seed: int = 0) -> dict:
    key_of = jax.random.split(jax.random.key(seed), 5)
    return {
        "parent_entries": draw_parent_entries(jax.random.fold_in(key_of[4], 71), 0),
        "updates": draw_updates(jax.random.fold_in(key_of[4], 71), 0),
        "block_maps": draw_block_maps(jax.random.fold_in(key_of[4], 71), 0),
        "live_blocks": plant((jax.random.randint(key_of[3], (SIBLINGS, CHILD // BLOCK), 0, 8) < 7).astype(jnp.int32), jax.random.fold_in(key_of[3], 1), 0, 1),
    }


HIGHEST = lax.Precision.HIGHEST

def inverse_factor(block):
    lower_part = jnp.linalg.cholesky(block)
    identity = jnp.eye(block.shape[0], dtype=block.dtype)
    return lax.linalg.triangular_solve(lower_part, identity, left_side=True, lower=True)

def reference(parent_entries, updates, block_maps, live_blocks):
    matrix_order = parent_entries.shape[0]
    parent_blocks = matrix_order // BLOCK
    child_blocks = updates.shape[1] // BLOCK
    matrix = parent_entries.reshape(parent_blocks, BLOCK, parent_blocks, BLOCK)
    for sibling in range(SIBLINGS):
        alive_blocks = live_blocks[sibling].astype(parent_entries.dtype)
        tile_set = updates[sibling].reshape(child_blocks, BLOCK, child_blocks, BLOCK)
        tile_set = tile_set * alive_blocks[:, None, None, None] * alive_blocks[None, None, :, None]
        targets = block_maps[sibling].astype(jnp.int32)
        matrix = matrix.at[targets[:, None], :, targets[None, :], :].add(jnp.transpose(tile_set, (0, 2, 1, 3)))
    matrix = matrix.reshape(matrix_order, matrix_order)
    row_ids = jnp.arange(matrix_order, dtype=jnp.int32)
    for panel_index in range(PANELS):
        start_col = panel_index * NB
        stop_col = start_col + NB
        inverse = inverse_factor(matrix[start_col:stop_col, start_col:stop_col])
        column = jnp.dot(matrix[:, start_col:stop_col], inverse.T, precision=HIGHEST)
        lower_mask = row_ids[:, None] >= (start_col + jnp.arange(NB, dtype=jnp.int32))[None, :]
        column = column * lower_mask.astype(column.dtype)
        below = column[stop_col:]
        matrix = matrix.at[stop_col:, stop_col:].add(-jnp.dot(below, below.T, precision=HIGHEST))
        matrix = matrix.at[:, start_col:stop_col].set(column)
        matrix = matrix.at[start_col:stop_col, stop_col:].set(0.0)
    return matrix
```

```python
import functools

import jax
import jax.numpy as jnp
from jax import lax
from jax.experimental import pallas as pl
from jax.experimental.pallas import tpu as pltpu
from jax.sharding import PartitionSpec as P

HIGHEST = lax.Precision.HIGHEST


def recip(d):
    r = pl.reciprocal(d, approx=True)
    r = r*(2.0-d*r)
    return r*(2.0-d*r)
def rsq(d):
    r = lax.rsqrt(d)
    return r*(1.5-0.5*d*r*r)
def diag_inverse(tile):
    rows=[tile[8*g:8*g+8,:] for g in range(16)]
    lane=lax.broadcasted_iota(jnp.int32,(8,128),1)
    sub=lax.broadcasted_iota(jnp.int32,(8,128),0)
    wide=lambda v: jnp.broadcast_to(v,(8,128))
    for m in range(16):
        o=8*m
        V=rows[m]
        b={(i,q): wide(V[i:i+1,o+q:o+q+1]) for i in range(8) for q in range(i+1)}
        cols={(g,q): wide(rows[g][:,o+q:o+q+1]) for g in range(m+1,16) for q in range(8)}
        inside=(lane>=o)&(lane<o+8)
        V=jnp.where(inside, jnp.where(lane-o==sub,1.0,0.0), V)
        v=[wide(V[i:i+1,:]) for i in range(8)]
        l={}; rd=[]
        for q in range(8):
            rd.append(recip(b[q,q]))
            for i in range(q+1,8):
                l[i,q]=b[i,q]*rd[q]
                for c in range(q+1,i+1):
                    b[i,c]=b[i,c]-l[i,q]*b[c,q]
                v[i]=v[i]-l[i,q]*v[q]
        t=[v[i]*rd[i] for i in range(8)]
        for i in range(6,-1,-1):
            for c in range(i+1,8):
                t[i]=t[i]-l[c,i]*t[c]
        new=v[0]*rsq(b[0,0])
        for i in range(1,8):
            new=jnp.where(sub==i, v[i]*rsq(b[i,i]), new)
        rows[m]=new
        for g in range(m+1,16):
            acc=jnp.where(inside,0.0,rows[g])
            for q in range(8):
                acc=acc-cols[g,q]*t[q]
            rows[g]=acc
    full=jnp.concatenate(rows,0)
    r=lax.broadcasted_iota(jnp.int32,(128,128),0); c=lax.broadcasted_iota(jnp.int32,(128,128),1)
    return jnp.where(c<=r, full, 0.0)
def factor_step(S, k):
    at=pl.ds(pl.multiple_of(k*128,128),128)
    inv=diag_inverse(S[at,at])
    r=lax.broadcasted_iota(jnp.int32,(128,128),0); c=lax.broadcasted_iota(jnp.int32,(128,128),1)
    S[at,at]=jnp.where(r==c,1.0,0.0)
    S[at,:]=jnp.dot(inv,S[at,:],precision=HIGHEST,preferred_element_type=jnp.float32)
    def body(i,_):
        ri=pl.ds(pl.multiple_of(i*128,128),128)
        L=S[at,ri]
        S[ri,at]=jnp.zeros((128,128),jnp.float32)
        S[ri,:]=S[ri,:]-lax.dot_general(L,S[at,:],(((0,),(0,)),((),())),precision=HIGHEST,preferred_element_type=jnp.float32)
        return 0
    lax.fori_loop(k+1,8,body,0)


def finish_body(place_ref, map_ref, live_ref, parent_ref, upd_ref, panel_ref, wt_ref, out_ref, whi, wlo, acc):
    i=pl.program_id(0)
    r=place_ref[0]; j=place_ref[1]
    @pl.when(i==0)
    def _():
        w=wt_ref[...]
        h=w.astype(jnp.bfloat16)
        whi[...]=h
        wlo[...]=(w-h.astype(jnp.float32)).astype(jnp.bfloat16)
    a=panel_ref[0]
    ahi=a.astype(jnp.bfloat16)
    alo=(a-ahi.astype(jnp.float32)).astype(jnp.bfloat16)
    dot=lambda x,y: jnp.dot(x,y,preferred_element_type=jnp.float32)
    acc[...]=dot(whi[...],ahi)+(dot(whi[...],alo)+dot(wlo[...],ahi))
    keep=jnp.where(j>=2,1.0,0.0).astype(jnp.float32)
    for c in range(4):
        for q in range(2):
            col=2*j+q
            bq=map_ref[c,col]-4*j
            lq=live_ref[c,col].astype(jnp.float32)*keep
            for p in range(2):
                row=16*r+2*i+p
                ap=map_ref[c,row]-4*(8*r+i)
                w=lq*live_ref[c,row].astype(jnp.float32)
                dst=(pl.ds(pl.multiple_of(bq*128,128),128),pl.ds(pl.multiple_of(ap*128,128),128))
                acc[dst]=acc[dst]+w*upd_ref[c,q*128:q*128+128,p*128:p*128+128]
    total=acc[...].T+keep*parent_ref[...]
    g=r*4096+i*512+lax.broadcasted_iota(jnp.int32,(512,512),0)
    s=j*512+lax.broadcasted_iota(jnp.int32,(512,512),1)
    out_ref[...]=jnp.where(g<jnp.minimum(s,1024),0.0,total)
def finish(place,maps,live,parent,upd,panel,wt):
    spec=pltpu.PrefetchScalarGridSpec(num_scalar_prefetch=3,grid=(8,),
      in_specs=[pl.BlockSpec((512,512),lambda i,*_:(i,0)),
                pl.BlockSpec((4,256,256),lambda i,*_:(0,0,i)),
                pl.BlockSpec((1,1024,512),lambda i,*_:(i,0,0)),
                pl.BlockSpec((512,1024),lambda i,*_:(0,0))],
      out_specs=pl.BlockSpec((512,512),lambda i,*_:(i,0)),
      scratch_shapes=[pltpu.VMEM((512,1024),jnp.bfloat16),pltpu.VMEM((512,1024),jnp.bfloat16),pltpu.VMEM((512,512),jnp.float32)])
    return pl.pallas_call(finish_body,grid_spec=spec,out_shape=jax.ShapeDtypeStruct((4096,512),jnp.float32),
      compiler_params=pltpu.CompilerParams(vmem_limit_bytes=48*2**20),
      cost_estimate=pl.CostEstimate(flops=3*2*4096*512*1024,bytes_accessed=45*2**20,transcendentals=0))(place,maps,live,parent,upd,panel,wt)


MESH = pl.DeviceIdType.MESH


class Links:
    def __init__(self, send_sem, recv_sem):
        self.send_sem, self.recv_sem, self.used = send_sem, recv_sem, 0
        self.pending = []

    def slot(self):
        self.used += 1
        return self.used - 1

    def copy(self, slot, source, target, device):
        return pltpu.make_async_remote_copy(
            src_ref=source,
            dst_ref=target,
            send_sem=self.send_sem.at[slot],
            recv_sem=self.recv_sem.at[slot],
            device_id=device,
            device_id_type=MESH,
        )

    def send(self, slot, ends):
        self.copy(slot, *ends()).start()
        self.pending.append((slot, ends))

    def landed(self, slot, region, device):
        self.copy(slot, region, region, device).wait_recv()

    def drain(self):
        for slot, ends in self.pending:
            self.copy(slot, *ends()).wait_send()
        self.pending = []


SLOTS = 96


def exchange_body(
    map_ref, live_ref, parent_ref, upd_ref, panel_ref, bulk_ref, wt_ref,
    upan, turned, top, square, first, second, send_sem, recv_sem, local_sem, part_send, part_recv,
):
    r = lax.axis_index("child")
    j = lax.axis_index("col")
    y, x, zl = j // 8, (j // 2) % 4, j % 2
    t = j % 8
    zh = r // 2
    core = r % 2
    links = Links(send_sem, recv_sem)
    is_root = (r == 0) & (j == 0)

    def col_at(ny, nx, nz):
        return ny * 8 + nx * 2 + nz

    def x_dev(step):
        return (r, col_at(y, (x + step) % 4, zl))

    def y_dev(step):
        return (r, col_at((y + step) % 4, x, zl))

    other_core = (r + 1 - 2 * core, j)

    panel_slots = [links.slot() for _ in range(4)]
    strip = upd_ref.at[0, :, pl.ds(0, 512)]
    for c in range(1, 4):
        @pl.when(r == c)
        def _(c=c):
            links.copy(panel_slots[c], strip, upan.at[c], (0, j)).start()

    bulk_slots = [links.slot() for _ in range(3)]
    partners = [r + 1 - 2 * core, (r + 2) % 4, 3 - r]

    def bulk_send(n):
        def ends():
            rows = pl.ds(pl.multiple_of(partners[n] * 2048, 2048), 2048)
            return upd_ref.at[0, :, rows], bulk_ref.at[r], (partners[n], j)

        links.send(bulk_slots[n], ends)

    own_rows = pl.ds(pl.multiple_of(r * 2048, 2048), 2048)
    own_bulk = pltpu.make_async_copy(upd_ref.at[0, :, own_rows], bulk_ref.at[r], local_sem.at[0])
    bulk_send(0)
    own_bulk.start()

    scatter_slots = [links.slot() for _ in range(4)]
    share_slots = [links.slot() for _ in range(3)]
    corner_slot = links.slot()

    def panel_part(piece, ny):
        return panel_ref.at[piece, ny]

    @pl.when(r == 0)
    def _():
        own = pltpu.make_async_copy(strip, upan.at[0], local_sem.at[1])
        head = pltpu.make_async_copy(parent_ref.at[pl.ds(0, 1024), :], top, local_sem.at[2])
        own.start()
        head.start()
        own.wait()
        for c in range(1, 4):
            links.landed(panel_slots[c], upan.at[c], (c, j))
        for c in range(4):
            for q in range(2):
                for p in range(4):
                    turned[c, p * 128:(p + 1) * 128, q * 128:(q + 1) * 128] = upan[
                        c, q * 128:(q + 1) * 128, p * 128:(p + 1) * 128
                    ].T
        head.wait()

        def place(step, _):
            a, b = step // 4, step % 4
            group = a // 4
            rows = pl.ds(pl.multiple_of(a * 128, 128), 128)
            cols = pl.ds(pl.multiple_of(b * 128, 128), 128)
            total = top[rows, cols]
            for c in range(4):
                for p in range(2):
                    row = 2 * group + p
                    row_weight = jnp.where(map_ref[c, row] == a, live_ref[c, row], 0)
                    source = pl.ds(pl.multiple_of(row * 128, 128), 128)
                    for q in range(2):
                        col = 2 * j + q
                        col_weight = jnp.where(map_ref[c, col] == 4 * j + b, live_ref[c, col], 0)
                        weight = (row_weight * col_weight).astype(jnp.float32)
                        total = total + weight * turned[c, source, q * 128:(q + 1) * 128]
            top[rows, cols] = total
            return 0

        lax.fori_loop(0, 32, place, 0)

    here = (r == 0) & (y == 0)

    @pl.when(here)
    def _():
        pltpu.make_async_copy(top.at[pl.ds(0, 256), :], panel_part(t, 0), local_sem.at[3]).start()

    for n in range(4):
        @pl.when((r == 0) & ((y + n) > 0))
        def _(n=n):
            links.copy(scatter_slots[n], top.at[pl.ds(n * 256, 256), :], panel_part(t, n), (y, n * 8 + t)).start()

    @pl.when((r == 0) & (j == 1))
    def _():
        links.copy(
            corner_slot, top.at[pl.ds(512, 512), :], square.at[pl.ds(512, 512), pl.ds(512, 512)], (0, 0)
        ).start()

    @pl.when(here)
    def _():
        pltpu.make_async_copy(top.at[pl.ds(0, 256), :], panel_part(t, 0), local_sem.at[3]).wait()

    for n in range(4):
        @pl.when((y == n) & ((r + y) > 0))
        def _(n=n):
            links.landed(scatter_slots[n], panel_part(t, n), (0, 8 * r + t))

    pair_slot = links.slot()
    links.send(pair_slot, lambda: (panel_part(t, y), panel_part(t, y), (r, j + 1 - 2 * zl)))

    @pl.when(r == 0)
    def _():
        links.copy(share_slots[0], top, top, (1, j)).start()
        links.copy(share_slots[1], top, top, (2, j)).start()

    @pl.when(is_root)
    def _():
        square[:, 0:512] = top[...]
        for a in range(4):
            for b in range(4):
                square[a * 128:(a + 1) * 128, 512 + b * 128:640 + b * 128] = top[
                    512 + b * 128:640 + b * 128, a * 128:(a + 1) * 128
                ].T
        links.landed(corner_slot, square.at[pl.ds(512, 512), pl.ds(512, 512)], (0, 1))

    OFFSETS = (0, 3, 1, 2)

    def pass_on(slot, region, device):
        def ends():
            here_and_there = region()
            return here_and_there, here_and_there, device()

        links.send(slot, ends)

    def item(kind, nx, ny):
        return panel_ref.at[pl.ds(2 * nx, 2), ny, pl.ds(kind * 128, 128), :]

    def half(kind, nx, ny, h):
        return panel_ref.at[2 * nx + h, ny, pl.ds(kind * 128, 128), :]

    def spot(kind, along, across):
        if kind == 0:
            return (x + along) % 4, (y + across) % 4
        return (x + across) % 4, (y + along) % 4

    def first_dev(kind, step):
        return x_dev(step) if kind == 0 else y_dev(step)

    def second_dev(kind, step):
        return y_dev(step) if kind == 0 else x_dev(step)

    one = [[links.slot() for _ in range(4)] for _ in range(2)]
    two = [{o: [links.slot() for _ in range(4)] for o in OFFSETS} for _ in range(2)]

    def second_send(o):
        for kind in range(2):
            region = lambda kind=kind: item(kind, *spot(kind, o, 0))
            pass_on(two[kind][o][0], region, functools.partial(second_dev, kind, 1))
            pass_on(two[kind][o][1], region, functools.partial(second_dev, kind, 3))

    def second_forward(o):
        for kind in range(2):
            links.landed(two[kind][o][0], item(kind, *spot(kind, o, 3)), second_dev(kind, 3))
            region = lambda kind=kind: half(kind, *spot(kind, o, 3), 0)
            pass_on(two[kind][o][2], region, functools.partial(second_dev, kind, 1))
            links.landed(two[kind][o][1], item(kind, *spot(kind, o, 1)), second_dev(kind, 1))
            region = lambda kind=kind: half(kind, *spot(kind, o, 1), 1)
            pass_on(two[kind][o][3], region, functools.partial(second_dev, kind, 3))

    def second_end(o):
        for kind in range(2):
            links.landed(two[kind][o][2], half(kind, *spot(kind, o, 2), 0), second_dev(kind, 3))
            links.landed(two[kind][o][3], half(kind, *spot(kind, o, 2), 1), second_dev(kind, 1))

    def event_pair():
        links.landed(pair_slot, panel_part(t + 1 - 2 * zl, y), (r, j + 1 - 2 * zl))
        for kind in range(2):
            region = functools.partial(item, kind, x, y)
            pass_on(one[kind][0], region, functools.partial(first_dev, kind, 1))
            pass_on(one[kind][1], region, functools.partial(first_dev, kind, 3))
        second_send(0)
        bulk_send(1)
        bulk_send(2)

    def event_near():
        for kind in range(2):
            links.landed(one[kind][0], item(kind, *spot(kind, 3, 0)), first_dev(kind, 3))
            region = lambda kind=kind: half(kind, *spot(kind, 3, 0), 0)
            pass_on(one[kind][2], region, functools.partial(first_dev, kind, 1))
            links.landed(one[kind][1], item(kind, *spot(kind, 1, 0)), first_dev(kind, 1))
            region = lambda kind=kind: half(kind, *spot(kind, 1, 0), 1)
            pass_on(one[kind][3], region, functools.partial(first_dev, kind, 3))
        second_send(3)
        second_send(1)

    def event_far():
        for kind in range(2):
            links.landed(one[kind][2], half(kind, *spot(kind, 2, 0), 0), first_dev(kind, 3))
            links.landed(one[kind][3], half(kind, *spot(kind, 2, 0), 1), first_dev(kind, 1))
        second_send(2)

    z = zh * 2 + zl
    part = y * 16 + x * 4 + z
    sets = (first, second)
    ring = [[links.slot() for _ in range(9)] for _ in range(2)]
    core_slots = [links.slot() for _ in range(2)]

    def chip(ny, nx, nz):
        return (2 * (nz // 2), col_at(ny, nx, nz % 2))

    def inverse_scatter(n):
        @pl.when(is_root)
        def _():
            def go(s, _):
                piece = sets[n].at[pl.ds(s, 1)]
                pltpu.make_async_remote_copy(
                    src_ref=piece, dst_ref=piece, send_sem=part_send.at[n, s], recv_sem=part_recv.at[n],
                    device_id=chip(s // 16, (s // 4) % 4, s % 4), device_id_type=MESH,
                ).start()
                return 0

            lax.fori_loop(1, 64, go, 0)

    def inverse_scatter_end(n):
        @pl.when(is_root)
        def _():
            def go(s, _):
                piece = sets[n].at[pl.ds(s, 1)]
                pltpu.make_async_remote_copy(
                    src_ref=piece, dst_ref=piece, send_sem=part_send.at[n, s], recv_sem=part_recv.at[n],
                    device_id=chip(s // 16, (s // 4) % 4, s % 4), device_id_type=MESH,
                ).wait_send()
                return 0

            lax.fori_loop(1, 64, go, 0)

    def span(n, level, nz, nx, ny):
        if level == 0:
            return sets[n].at[pl.ds(ny * 16 + nx * 4 + nz, 1)]
        if level == 1:
            return sets[n].at[pl.ds(ny * 16 + nx * 4, 4)]
        return sets[n].at[pl.ds(ny * 16, 16)]

    def moved(level, step):
        if level == 0:
            return (z + step) % 4, x, y
        if level == 1:
            return z, (x + step) % 4, y
        return z, x, (y + step) % 4

    def level_copies(n, level, act):
        for step in range(1, 4):
            nz, nx, ny = moved(level, step)

            @pl.when((core == 0) & (nz + nx + ny > 0))
            def _(step=step, nz=nz, nx=nx, ny=ny):
                region = span(n, level, z, x, y)
                act(links.copy(ring[n][level * 3 + step - 1], region, region, chip(ny, nx, nz)))

    def level_send(n, level):
        level_copies(n, level, lambda copy: copy.start())

    def level_end(n, level):
        @pl.when((core == 0) & (part > 0))
        def _():
            for step in range(1, 4):
                nz, nx, ny = moved(level, 4 - step)
                links.landed(ring[n][level * 3 + step - 1], span(n, level, nz, nx, ny), chip(ny, nx, nz))

    def part_end(n):
        @pl.when((core == 0) & (part > 0))
        def _():
            piece = sets[n].at[pl.ds(part, 1)]
            pltpu.make_async_remote_copy(
                src_ref=piece, dst_ref=piece, send_sem=part_send.at[n, 0], recv_sem=part_recv.at[n],
                device_id=(0, 0), device_id_type=MESH,
            ).wait_recv()

    def core_send(n):
        @pl.when(core == 0)
        def _():
            links.copy(core_slots[n], sets[n], sets[n], (r + 1, j)).start()

    def core_end(n):
        @pl.when(core == 1)
        def _():
            links.landed(core_slots[n], sets[n], (r - 1, j))

    def event_share():
        @pl.when(r == 1)
        def _():
            links.landed(share_slots[0], top, (0, j))

        @pl.when(r == 2)
        def _():
            links.landed(share_slots[1], top, (0, j))
            links.copy(share_slots[2], top, top, (3, j)).start()

        @pl.when(r == 3)
        def _():
            links.landed(share_slots[2], top, (2, j))

    def times(a, b, dims):
        return lax.dot_general(a, b, (dims, ((), ())), precision=HIGHEST, preferred_element_type=jnp.float32)

    def weights_first():
        wt_ref[:, 512:1024] = jnp.zeros((512, 512), jnp.float32)

        @pl.when(j == 0)
        def _():
            wt_ref[:, 0:512] = first[...].reshape(512, 512)

        @pl.when(j == 1)
        def _():
            wt_ref[:, 0:512] = jnp.zeros((512, 512), jnp.float32)

        @pl.when(j >= 2)
        def _():
            inverse = first[...].reshape(512, 512)
            solved = times(inverse, top[0:512, :], ((1,), (0,)))
            wt_ref[:, 0:512] = -times(solved, inverse, ((0,), (0,)))

    def weights_second():
        @pl.when(j == 1)
        def _():
            wt_ref[...] = second[...].reshape(512, 1024)

        @pl.when(j >= 2)
        def _():
            inverse = second[...].reshape(512, 1024)
            solved = times(inverse, top[...], ((1,), (0,)))
            wt_ref[...] = wt_ref[...] - times(solved, inverse, ((0,), (0,)))

    def keep_inverse(n):
        @pl.when(is_root)
        def _():
            width = 512 * (n + 1)
            rows = n * 512 + lax.broadcasted_iota(jnp.int32, (512, width), 0)
            cols = lax.broadcasted_iota(jnp.int32, (512, width), 1)
            kept = jnp.where(cols <= rows, square[n * 512:(n + 1) * 512, 0:width], 0.0)
            sets[n][...] = kept.reshape(64, 8, width)

    plan = {
        0: [event_pair],
        1: [],
        2: [event_near],
        3: [functools.partial(keep_inverse, 0), functools.partial(inverse_scatter, 0), event_far, event_share],
        4: [functools.partial(part_end, 0), functools.partial(level_send, 0, 0),
            functools.partial(second_forward, 0),
            functools.partial(level_end, 0, 0), functools.partial(level_send, 0, 1)],
        5: [functools.partial(second_forward, 3), functools.partial(second_forward, 1),
            functools.partial(level_end, 0, 1), functools.partial(level_send, 0, 2)],
        6: [functools.partial(second_forward, 2),
            functools.partial(level_end, 0, 2), functools.partial(core_send, 0),
            functools.partial(core_end, 0), weights_first],
        7: [functools.partial(keep_inverse, 1), functools.partial(inverse_scatter, 1)],
    }

    def step(k, _):
        @pl.when(is_root)
        def _():
            factor_step(square, k)

        for n, events in plan.items():
            if events:
                @pl.when(k == n)
                def _(events=events):
                    for event in events:
                        event()

        return 0

    lax.fori_loop(0, 8, step, 0)
    part_end(1)
    level_send(1, 0)
    level_end(1, 0)
    level_send(1, 1)
    level_end(1, 1)
    level_send(1, 2)
    level_end(1, 2)
    core_send(1)
    core_end(1)
    weights_second()
    for o in OFFSETS:
        second_end(o)
    own_bulk.wait()
    for n in range(3):
        links.landed(bulk_slots[n], bulk_ref.at[partners[n]], (partners[n], j))
    links.drain()
    for c in range(1, 4):
        @pl.when(r == c)
        def _(c=c):
            links.copy(panel_slots[c], strip, upan.at[c], (0, j)).wait_send()
    for n in range(4):
        @pl.when((r == 0) & ((y + n) > 0))
        def _(n=n):
            links.copy(scatter_slots[n], top.at[pl.ds(n * 256, 256), :], panel_part(t, n), (y, n * 8 + t)).wait_send()

    @pl.when((r == 0) & (j == 1))
    def _():
        links.copy(
            corner_slot, top.at[pl.ds(512, 512), :], square.at[pl.ds(512, 512), pl.ds(512, 512)], (0, 0)
        ).wait_send()

    @pl.when(r == 0)
    def _():
        links.copy(share_slots[0], top, top, (1, j)).wait_send()
        links.copy(share_slots[1], top, top, (2, j)).wait_send()

    @pl.when(r == 2)
    def _():
        links.copy(share_slots[2], top, top, (3, j)).wait_send()

    for n in range(2):
        inverse_scatter_end(n)

        for level in range(3):
            level_copies(n, level, lambda copy: copy.wait_send())

        @pl.when(core == 0)
        def _(n=n):
            links.copy(core_slots[n], sets[n], sets[n], (r + 1, j)).wait_send()


def exchange(maps, live, parent, updates):
    hbm = pl.BlockSpec(memory_space=pl.ANY)
    smem = pl.BlockSpec(memory_space=pltpu.SMEM)
    return pl.pallas_call(
        exchange_body,
        out_shape=(
            jax.ShapeDtypeStruct((8, 4, 256, 512), jnp.float32),
            jax.ShapeDtypeStruct((4, 256, 2048), jnp.float32),
            jax.ShapeDtypeStruct((512, 1024), jnp.float32),
        ),
        in_specs=[smem, smem, hbm, hbm],
        out_specs=(hbm, hbm, pl.BlockSpec(memory_space=pltpu.VMEM)),
        scratch_shapes=[
            pltpu.VMEM((4, 256, 512), jnp.float32),
            pltpu.VMEM((4, 512, 256), jnp.float32),
            pltpu.VMEM((1024, 512), jnp.float32),
            pltpu.VMEM((1024, 1024), jnp.float32),
            pltpu.VMEM((64, 8, 512), jnp.float32),
            pltpu.VMEM((64, 8, 1024), jnp.float32),
            pltpu.SemaphoreType.DMA((SLOTS,)),
            pltpu.SemaphoreType.DMA((SLOTS,)),
            pltpu.SemaphoreType.DMA((4,)),
            pltpu.SemaphoreType.DMA((2, 64)),
            pltpu.SemaphoreType.DMA((2,)),
        ],
        compiler_params=pltpu.CompilerParams(has_side_effects=True, vmem_limit_bytes=40 * 2**20),
    )(maps, live, parent, updates)


def per_device(parent, updates, maps, live):
    panel, bulk, wt = exchange(maps, live, parent, updates)
    place = jnp.stack([lax.axis_index("child"), lax.axis_index("col")]).astype(jnp.int32)
    return finish(place, maps, live, parent, bulk, panel.reshape(8, 1024, 512), wt)


def solution(mesh):
    in_specs = (P("child", "col"), P("child", "col", None), P(), P())
    return jax.shard_map(
        per_device, mesh=mesh, in_specs=in_specs, out_specs=P("child", "col"), check_vma=False
    )
```

```python
import functools

import jax
import jax.numpy as jnp
from jax import lax
from jax.experimental import pallas as pl
from jax.experimental.pallas import tpu as pltpu
from jax.sharding import PartitionSpec as P

HIGHEST = lax.Precision.HIGHEST


def recip(d):
    r = pl.reciprocal(d, approx=True)
    return r*(2.0-d*r)
def rsq(d):
    r = lax.rsqrt(d)
    return r*(1.5-0.5*d*r*r)
def diag_inverse(tile):
    rows=[tile[8*g:8*g+8,:] for g in range(16)]
    lane=lax.broadcasted_iota(jnp.int32,(8,128),1)
    sub=lax.broadcasted_iota(jnp.int32,(8,128),0)
    wide=lambda v: jnp.broadcast_to(v,(8,128))
    for m in range(16):
        o=8*m
        V=rows[m]
        inside=(lane>=o)&(lane<o+8)
        b={(i,q): wide(V[i:i+1,o+q:o+q+1]) for i in range(8) for q in range(i+1)}
        cols={(g,q): wide(rows[g][:,o+q:o+q+1]) for g in range(m+1,16) for q in range(8)}
        V=jnp.where(inside, jnp.where(lane-o==sub,1.0,0.0), V)
        v=[wide(V[i:i+1,:]) for i in range(8)]
        if m<15:
            after=jnp.where(inside,0.0,rows[m+1])
            ce=[cols[m+1,q] for q in range(8)]
        l={}; rd=[]
        for q in range(8):
            rd.append(recip(b[q,q]))
            for i in range(q+1,8):
                for c in range(q+1,i+1):
                    b[i,c]=b[i,c]-(b[i,q]*b[c,q])*rd[q]
                l[i,q]=b[i,q]*rd[q]
                v[i]=v[i]-l[i,q]*v[q]
            if m<15:
                times=ce[q]*rd[q]
                after=after-times*v[q]
                for c in range(q+1,8):
                    ce[c]=ce[c]-times*b[c,q]
        if m<15:
            rows[m+1]=after
        new=v[0]*rsq(b[0,0])
        for i in range(1,8):
            new=jnp.where(sub==i, v[i]*rsq(b[i,i]), new)
        rows[m]=new
        if m<14:
            t=[v[i]*rd[i] for i in range(8)]
            for i in range(6,-1,-1):
                for c in range(i+1,8):
                    t[i]=t[i]-l[c,i]*t[c]
            for g in range(m+2,16):
                acc=jnp.where(inside,0.0,rows[g])
                for q in range(8):
                    acc=acc-cols[g,q]*t[q]
                rows[g]=acc
    full=jnp.concatenate(rows,0)
    r=lax.broadcasted_iota(jnp.int32,(128,128),0); c=lax.broadcasted_iota(jnp.int32,(128,128),1)
    return jnp.where(c<=r, full, 0.0)
def block_at(k):
    return pl.ds(pl.multiple_of(k*128,128),128)
def factor_start(S,inv):
    inv[...]=diag_inverse(S[0:128,0:128])
def factor_step(S,inv,k):
    at=block_at(k)
    r=lax.broadcasted_iota(jnp.int32,(128,128),0); c=lax.broadcasted_iota(jnp.int32,(128,128),1)
    S[at,at]=jnp.where(r==c,1.0,0.0)
    row=jnp.dot(inv[...],S[at,:],precision=HIGHEST,preferred_element_type=jnp.float32)
    S[at,:]=row
    def clear(i,_):
        S[block_at(i),at]=jnp.zeros((128,128),jnp.float32)
        return 0
    lax.fori_loop(k+1,8,clear,0)
    @pl.when(k<7)
    def _():
        nx=block_at(k+1)
        tn=lambda a,b: lax.dot_general(a,b,(((0,),(0,)),((),())),precision=HIGHEST,preferred_element_type=jnp.float32)
        S[nx,:]=S[nx,:]-tn(S[at,nx],S[at,:])
        tile=S[nx,nx]
        cols=lax.broadcasted_iota(jnp.int32,(128,1024),1)
        full=S[at,:]
        left=jnp.where(cols>=(k+2)*128,full,0.0)
        inv[...]=diag_inverse(tile)
        for g in range(2,8):
            S[g*128:g*128+128,:]=S[g*128:g*128+128,:]-tn(left[:,g*128:g*128+128],full)


def finish_body(place_ref, map_ref, live_ref, parent_ref, upd_ref, panel_ref, wt_ref, out_ref, whi, wlo, acc):
    i=pl.program_id(0)
    r=place_ref[0]; j=place_ref[1]
    @pl.when(i==0)
    def _():
        w=wt_ref[...]
        h=w.astype(jnp.bfloat16)
        whi[...]=h
        wlo[...]=(w-h.astype(jnp.float32)).astype(jnp.bfloat16)
    a=panel_ref[0]
    ahi=a.astype(jnp.bfloat16)
    alo=(a-ahi.astype(jnp.float32)).astype(jnp.bfloat16)
    dot=lambda x,y: jnp.dot(x,y,preferred_element_type=jnp.float32)
    acc[...]=dot(whi[...],ahi)+(dot(whi[...],alo)+dot(wlo[...],ahi))
    keep=jnp.where(j>=2,1.0,0.0).astype(jnp.float32)
    for c in range(4):
        for q in range(2):
            col=2*j+q
            bq=map_ref[c,col]-4*j
            lq=live_ref[c,col].astype(jnp.float32)*keep
            for p in range(2):
                row=16*r+2*i+p
                ap=map_ref[c,row]-4*(8*r+i)
                w=lq*live_ref[c,row].astype(jnp.float32)
                dst=(pl.ds(pl.multiple_of(bq*128,128),128),pl.ds(pl.multiple_of(ap*128,128),128))
                acc[dst]=acc[dst]+w*upd_ref[c,q*128:q*128+128,p*128:p*128+128]
    total=acc[...].T+keep*parent_ref[...]
    g=r*4096+i*512+lax.broadcasted_iota(jnp.int32,(512,512),0)
    s=j*512+lax.broadcasted_iota(jnp.int32,(512,512),1)
    out_ref[...]=jnp.where(g<jnp.minimum(s,1024),0.0,total)
def finish(place,maps,live,parent,upd,panel,wt):
    spec=pltpu.PrefetchScalarGridSpec(num_scalar_prefetch=3,grid=(8,),
      in_specs=[pl.BlockSpec((512,512),lambda i,*_:(i,0)),
                pl.BlockSpec((4,256,256),lambda i,*_:(0,0,i)),
                pl.BlockSpec((1,1024,512),lambda i,*_:(i,0,0)),
                pl.BlockSpec((512,1024),lambda i,*_:(0,0))],
      out_specs=pl.BlockSpec((512,512),lambda i,*_:(i,0)),
      scratch_shapes=[pltpu.VMEM((512,1024),jnp.bfloat16),pltpu.VMEM((512,1024),jnp.bfloat16),pltpu.VMEM((512,512),jnp.float32)])
    return pl.pallas_call(finish_body,grid_spec=spec,out_shape=jax.ShapeDtypeStruct((4096,512),jnp.float32),
      compiler_params=pltpu.CompilerParams(vmem_limit_bytes=48*2**20),
      cost_estimate=pl.CostEstimate(flops=3*2*4096*512*1024,bytes_accessed=45*2**20,transcendentals=0))(place,maps,live,parent,upd,panel,wt)


MESH = pl.DeviceIdType.MESH


class Links:
    def __init__(self, send_sem, recv_sem):
        self.send_sem, self.recv_sem, self.used = send_sem, recv_sem, 0
        self.pending = []

    def slot(self):
        self.used += 1
        return self.used - 1

    def slots(self, count):
        self.used += count
        return self.used - count

    def copy(self, slot, source, target, device):
        return pltpu.make_async_remote_copy(
            src_ref=source,
            dst_ref=target,
            send_sem=self.send_sem.at[slot],
            recv_sem=self.recv_sem.at[slot],
            device_id=device,
            device_id_type=MESH,
        )

    def send(self, slot, ends):
        self.copy(slot, *ends()).start()
        self.pending.append((slot, ends))

    def landed(self, slot, region, device):
        self.copy(slot, region, region, device).wait_recv()

    def drain(self):
        for slot, ends in self.pending:
            self.copy(slot, *ends()).wait_send()
        self.pending = []


SLOTS = 128
BULK = (0, 2, 1, 2, 1, 2)
WIDTHS = (768, 512)
WHERE = ((0, 0), (0, 128), (0, 384), (1, 0))


def exchange_body(
    map_ref, live_ref, parent_ref, upd_ref, panel_ref, bulk_ref, wt_ref,
    raw, turned, chunk, top, square, corner, inverse, weight, set_0, set_1,
    send_sem, recv_sem, local_sem, part_send, part_recv,
):
    r = lax.axis_index("child")
    j = lax.axis_index("col")
    y, x, zl = j // 8, (j // 2) % 4, j % 2
    t = j % 8
    zh = r // 2
    core = r % 2
    links = Links(send_sem, recv_sem)
    is_root = (r == 0) & (j == 0)
    source_col = 8 * r + t

    def col_at(ny, nx, nz):
        return ny * 8 + nx * 2 + nz

    def x_dev(step):
        return (r, col_at(y, (x + step) % 4, zl))

    def y_dev(step):
        return (r, col_at((y + step) % 4, x, zl))

    def panel_part(piece, ny):
        return panel_ref.at[piece, ny]

    head_slot = links.slots(4)
    strip_slot = links.slots(16)

    def strip(n):
        return upd_ref.at[0, :, pl.ds(256 * (n // 2), 256)]

    def head_copy(n):
        return links.copy(head_slot + n, parent_ref.at[pl.ds(256 * n, 256), :], chunk, (y, n * 8 + t))

    def strip_copy(n):
        return links.copy(strip_slot + 4 * r + n, strip(n), raw.at[r], (y, n * 8 + t))

    def panel_sends(act):
        for n in range(4):
            @pl.when((r != y) | (y != n))
            def _(n=n):
                act(strip_copy(n))

            @pl.when((r == 0) & (y + n > 0))
            def _(n=n):
                act(head_copy(n))

    panel_sends(lambda copy: copy.start())
    own_head = pltpu.make_async_copy(parent_ref.at[pl.ds(0, 256), :], chunk, local_sem.at[1])

    def own_strip():
        part = upd_ref.at[0, :, pl.ds(pl.multiple_of(256 * (y // 2), 256), 256)]
        return pltpu.make_async_copy(part, raw.at[r], local_sem.at[2])

    @pl.when((r == 0) & (y == 0))
    def _():
        own_head.start()

    @pl.when(r == y)
    def _():
        own_strip().start()

    partners = [r + 1 - 2 * core, (r + 2) % 4, 3 - r]
    bulk_slot = links.slot()
    bulk_queue = [(n, m, links.slot()) for m in range(4) for n in (1, 2)]
    bulk_all = list(bulk_queue)

    def bulk_send():
        def ends():
            rows = pl.ds(pl.multiple_of(partners[0] * 2048, 2048), 2048)
            return upd_ref.at[0, :, rows], bulk_ref.at[r], (partners[0], j)

        links.send(bulk_slot, ends)

    def bulk_some(count):
        for _ in range(count):
            n, m, slot = bulk_queue.pop(0)

            def ends(n=n, m=m):
                rows = pl.ds(pl.multiple_of(partners[n] * 2048 + 512 * m, 512), 512)
                return upd_ref.at[0, :, rows], bulk_ref.at[r, :, pl.ds(512 * m, 512)], (partners[n], j)

            links.send(slot, ends)

    own_rows = pl.ds(pl.multiple_of(r * 2048, 2048), 2048)
    own_bulk = pltpu.make_async_copy(upd_ref.at[0, :, own_rows], bulk_ref.at[r], local_sem.at[0])
    bulk_some(BULK[0])
    weight[...] = jnp.zeros((512, 1024), jnp.float32)

    @pl.when(r == y)
    def _():
        own_strip().wait()

    for c in range(4):
        @pl.when((r != c) | (r != y))
        def _(c=c):
            links.landed(strip_slot + 4 * c + y, raw.at[c], (c, source_col))
        for q in range(2):
            for p in range(2):
                turned[c, p * 128:(p + 1) * 128, q * 128:(q + 1) * 128] = raw[
                    c, q * 128:(q + 1) * 128, p * 128:(p + 1) * 128
                ].T

    @pl.when((r == 0) & (y == 0))
    def _():
        own_head.wait()

    @pl.when((r > 0) | (y > 0))
    def _():
        links.landed(head_slot + y, chunk, (0, source_col))

    def place(step, _):
        a, b = step // 4, step % 4
        rows = pl.ds(pl.multiple_of(a * 128, 128), 128)
        cols = pl.ds(pl.multiple_of(b * 128, 128), 128)
        total = chunk[rows, cols]
        for c in range(4):
            for p in range(2):
                row = 2 * (y // 2) + p
                row_weight = jnp.where(map_ref[c, row] == 2 * y + a, live_ref[c, row], 0)
                for q in range(2):
                    col = 2 * source_col + q
                    col_weight = jnp.where(map_ref[c, col] == 4 * source_col + b, live_ref[c, col], 0)
                    both = (row_weight * col_weight).astype(jnp.float32)
                    total = total + both * turned[c, p * 128:(p + 1) * 128, q * 128:(q + 1) * 128]
        chunk[rows, cols] = total
        return 0

    lax.fori_loop(0, 8, place, 0)

    pivot_slot = links.slots(8)

    def pivot_part(side, n):
        if side == 0:
            return square.at[pl.ds(pl.multiple_of(n * 256, 256), 256), pl.ds(0, 512)]
        return corner.at[pl.ds(pl.multiple_of(n * 256 - 512, 256), 256), :]

    def pivot_sends(act):
        for side in range(2):
            @pl.when((r == 0) & (t == side) & (y > side))
            def _(side=side):
                act(links.copy(pivot_slot + 4 * side + y, chunk, pivot_part(side, y), (0, 0)))

    pivot_sends(lambda copy: copy.start())
    pair_slot = links.slot()
    links.send(pair_slot, lambda: (chunk, panel_part(t, y), (r, j + 1 - 2 * zl)))
    own_chunk = pltpu.make_async_copy(chunk, panel_part(t, y), local_sem.at[1])
    own_chunk.start()
    bulk_send()
    own_bulk.start()

    def root_square():
        square[0:256, 0:512] = chunk[...]
        square[512:1024, 512:1024] = jnp.zeros((512, 512), jnp.float32)
        for n in range(1, 4):
            links.landed(pivot_slot + n, pivot_part(0, n), (0, 8 * n))
        for a in range(4):
            for b in range(4):
                square[a * 128:(a + 1) * 128, 512 + b * 128:640 + b * 128] = square[
                    512 + b * 128:640 + b * 128, a * 128:(a + 1) * 128
                ].T
        factor_start(square, inverse)

    def root_corner():
        for n in range(2, 4):
            links.landed(pivot_slot + 4 + n, pivot_part(1, n), (0, 8 * n + 1))
        square[512:1024, 512:1024] = square[512:1024, 512:1024] + corner[...]

    OFFSETS = (0, 3, 1, 2)

    def pass_on(slot, region, device):
        def ends():
            here_and_there = region()
            return here_and_there, here_and_there, device()

        links.send(slot, ends)

    def item(kind, nx, ny):
        return panel_ref.at[pl.ds(2 * nx, 2), ny, pl.ds(kind * 128, 128), :]

    def half(kind, nx, ny, h):
        return panel_ref.at[2 * nx + h, ny, pl.ds(kind * 128, 128), :]

    def spot(kind, along, across):
        if kind == 0:
            return (x + along) % 4, (y + across) % 4
        return (x + across) % 4, (y + along) % 4

    def first_dev(kind, step):
        return x_dev(step) if kind == 0 else y_dev(step)

    def second_dev(kind, step):
        return y_dev(step) if kind == 0 else x_dev(step)

    one = [[links.slot() for _ in range(4)] for _ in range(2)]
    two = [{o: [links.slot() for _ in range(4)] for o in OFFSETS} for _ in range(2)]

    def second_send(o):
        for kind in range(2):
            region = lambda kind=kind: item(kind, *spot(kind, o, 0))
            pass_on(two[kind][o][0], region, functools.partial(second_dev, kind, 1))
            pass_on(two[kind][o][1], region, functools.partial(second_dev, kind, 3))

    def second_forward(o):
        for kind in range(2):
            links.landed(two[kind][o][0], item(kind, *spot(kind, o, 3)), second_dev(kind, 3))
            region = lambda kind=kind: half(kind, *spot(kind, o, 3), 0)
            pass_on(two[kind][o][2], region, functools.partial(second_dev, kind, 1))
            links.landed(two[kind][o][1], item(kind, *spot(kind, o, 1)), second_dev(kind, 1))
            region = lambda kind=kind: half(kind, *spot(kind, o, 1), 1)
            pass_on(two[kind][o][3], region, functools.partial(second_dev, kind, 3))

    def second_end(o):
        for kind in range(2):
            links.landed(two[kind][o][2], half(kind, *spot(kind, o, 2), 0), second_dev(kind, 3))
            links.landed(two[kind][o][3], half(kind, *spot(kind, o, 2), 1), second_dev(kind, 1))

    def event_pair():
        own_chunk.wait()
        links.landed(pair_slot, panel_part(t + 1 - 2 * zl, y), (r, j + 1 - 2 * zl))
        for kind in range(2):
            region = functools.partial(item, kind, x, y)
            pass_on(one[kind][0], region, functools.partial(first_dev, kind, 1))
            pass_on(one[kind][1], region, functools.partial(first_dev, kind, 3))
        second_send(0)
        bulk_some(BULK[1])

    def event_near():
        for kind in range(2):
            links.landed(one[kind][0], item(kind, *spot(kind, 3, 0)), first_dev(kind, 3))
            region = lambda kind=kind: half(kind, *spot(kind, 3, 0), 0)
            pass_on(one[kind][2], region, functools.partial(first_dev, kind, 1))
            links.landed(one[kind][1], item(kind, *spot(kind, 1, 0)), first_dev(kind, 1))
            region = lambda kind=kind: half(kind, *spot(kind, 1, 0), 1)
            pass_on(one[kind][3], region, functools.partial(first_dev, kind, 3))
        second_send(3)
        second_send(1)

    def event_far():
        for kind in range(2):
            links.landed(one[kind][2], half(kind, *spot(kind, 2, 0), 0), first_dev(kind, 3))
            links.landed(one[kind][3], half(kind, *spot(kind, 2, 0), 1), first_dev(kind, 1))
        second_send(2)

    home = r == y
    across = r == (y + 2) % 4
    home_core = r == y + 1 - 2 * (y % 2)
    share_slots = [links.slot() for _ in range(3)]

    def own_top():
        return pltpu.make_async_copy(panel_ref.at[t], top, local_sem.at[2])

    def share_copies():
        return (
            links.copy(share_slots[0], panel_ref.at[t], top, ((r + 2) % 4, j)),
            links.copy(share_slots[1], panel_ref.at[t], top, (r + 1 - 2 * core, j)),
        )

    def share_core():
        return links.copy(share_slots[2], top, top, (r + 1 - 2 * core, j))

    def event_share():
        second_end(0)

        @pl.when(home)
        def _():
            for copy in share_copies():
                copy.start()
            own_top().start()

    def event_share_across():
        @pl.when(home)
        def _():
            own_top().wait()

        @pl.when(home_core)
        def _():
            links.landed(share_slots[1], top, (y, j))

        @pl.when(across)
        def _():
            links.landed(share_slots[0], top, (y, j))
            share_core().start()

    def event_share_end():
        @pl.when(jnp.logical_not(home | home_core | across))
        def _():
            links.landed(share_slots[2], top, ((y + 2) % 4, j))

    z = zh * 2 + zl
    part = y * 16 + x * 4 + z
    sets = (set_0, set_1)
    ring = [[links.slot() for _ in range(9)] for _ in range(2)]
    core_slots = [links.slot() for _ in range(2)]

    def chip(ny, nx, nz):
        return (2 * (nz // 2), col_at(ny, nx, nz % 2))

    def part_copy(n, s, device):
        piece = sets[n].at[pl.ds(s, 1)]
        return pltpu.make_async_remote_copy(
            src_ref=piece, dst_ref=piece, send_sem=part_send.at[n, s], recv_sem=part_recv.at[n],
            device_id=device, device_id_type=MESH,
        )

    def part_sends(n, act):
        @pl.when(is_root)
        def _():
            def go(s, _):
                act(part_copy(n, s, chip(s // 16, (s // 4) % 4, s % 4)))
                return 0

            lax.fori_loop(1, 64, go, 0)

    def span(n, level, nz, nx, ny):
        if level == 0:
            return sets[n].at[pl.ds(ny * 16 + nx * 4 + nz, 1)]
        if level == 1:
            return sets[n].at[pl.ds(ny * 16 + nx * 4, 4)]
        return sets[n].at[pl.ds(ny * 16, 16)]

    def moved(level, step):
        if level == 0:
            return (z + step) % 4, x, y
        if level == 1:
            return z, (x + step) % 4, y
        return z, x, (y + step) % 4

    def level_copies(n, level, act):
        for step in range(1, 4):
            nz, nx, ny = moved(level, step)

            @pl.when((core == 0) & (nz + nx + ny > 0))
            def _(step=step, nz=nz, nx=nx, ny=ny):
                region = span(n, level, z, x, y)
                act(links.copy(ring[n][level * 3 + step - 1], region, region, chip(ny, nx, nz)))

    def level_end(n, level):
        @pl.when((core == 0) & (part > 0))
        def _():
            for step in range(1, 4):
                nz, nx, ny = moved(level, 4 - step)
                links.landed(ring[n][level * 3 + step - 1], span(n, level, nz, nx, ny), chip(ny, nx, nz))

    def core_copy(n):
        return links.copy(core_slots[n], sets[n], sets[n], (r + 1, j))

    def keep(n):
        half = 128 * (n + 1)
        which, at = WHERE[n]
        rows = n * 256 + lax.broadcasted_iota(jnp.int32, (256, half), 0)
        cols = lax.broadcasted_iota(jnp.int32, (256, half), 1)
        for h in range(2):
            kept = square[n * 256:(n + 1) * 256, h * half:(h + 1) * half]
            kept = jnp.where(cols + h * half <= rows, kept, 0.0)
            sets[which][h * 32:(h + 1) * 32, :, at:at + half] = kept.reshape(32, 8, half)

    def leave(n):
        @pl.when(is_root)
        def _():
            for m in ((0, 1, 2), (3,))[n]:
                keep(m)

        part_sends(n, lambda copy: copy.start())

    def over_z(n):
        @pl.when((core == 0) & (part > 0))
        def _():
            part_copy(n, part, (0, 0)).wait_recv()

        level_copies(n, 0, lambda copy: copy.start())

    def over_x(n):
        level_end(n, 0)
        level_copies(n, 1, lambda copy: copy.start())

    def over_y(n):
        level_end(n, 1)
        level_copies(n, 2, lambda copy: copy.start())

    def over_core(n):
        level_end(n, 2)

        @pl.when(core == 0)
        def _():
            core_copy(n).start()

    def split(a):
        high = a.astype(jnp.bfloat16)
        return high, (a - high.astype(jnp.float32)).astype(jnp.bfloat16)

    def times(a, b, dims):
        dot = lambda u, v: lax.dot_general(u, v, (dims, ((), ())), preferred_element_type=jnp.float32)
        return dot(a[0], b[0]) + (dot(a[0], b[1]) + dot(a[1], b[0]))

    def weigh(n):
        half = 128 * (n + 1)
        which, at = WHERE[n]
        width = 2 * half

        def lower():
            return jnp.concatenate(
                [sets[which][h * 32:(h + 1) * 32, :, at:at + half].reshape(256, half) for h in range(2)], axis=1
            )

        @pl.when(j == n // 2)
        def _():
            weight[n % 2 * 256:(n % 2 + 1) * 256, 0:width] = lower()

        @pl.when(j >= 2)
        def _():
            part_of = split(lower())
            solved = times(part_of, split(top[0:n + 1].reshape(width, 512)), ((1,), (0,)))
            weight[:, 0:width] = weight[:, 0:width] - times(split(solved), part_of, ((0,), (0,)))

    def arrive(n):
        @pl.when(core == 1)
        def _():
            links.landed(core_slots[n], sets[n], (r - 1, j))

        for m in ((0, 1, 2), (3,))[n]:
            weigh(m)

    do = functools.partial
    plan = {
        0: [event_far],
        1: [do(second_forward, 0), do(bulk_some, BULK[3])],
        3: [do(second_forward, 3)],
        4: [event_share],
        5: [do(leave, 0), do(second_forward, 1), do(over_z, 0), do(bulk_some, BULK[4])],
        6: [do(over_x, 0)],
        7: [do(leave, 1), do(over_y, 0), do(over_z, 1), do(second_forward, 2), do(over_x, 1)],
    }

    def step(k, _):
        @pl.when(is_root & (k == 3))
        def _():
            root_corner()

        @pl.when(is_root)
        def _():
            factor_step(square, inverse, k)

        for n, events in plan.items():
            @pl.when(k == n)
            def _(events=events):
                for event in events:
                    event()

        return 0

    event_pair()

    @pl.when(is_root)
    def _():
        root_square()

    event_near()
    bulk_some(BULK[2])
    lax.fori_loop(0, 8, step, 0)
    event_share_across()
    bulk_some(BULK[5])
    over_core(0)
    over_y(1)
    event_share_end()
    arrive(0)
    over_core(1)
    arrive(1)
    out = pltpu.make_async_copy(weight, wt_ref, local_sem.at[1])
    out.start()
    for o in OFFSETS[1:]:
        second_end(o)
    own_bulk.wait()
    links.landed(bulk_slot, bulk_ref.at[partners[0]], (partners[0], j))
    for n, m, slot in bulk_all:
        links.landed(slot, bulk_ref.at[partners[n], :, pl.ds(512 * m, 512)], (partners[n], j))
    links.drain()
    panel_sends(lambda copy: copy.wait_send())
    pivot_sends(lambda copy: copy.wait_send())

    @pl.when(home)
    def _():
        for copy in share_copies():
            copy.wait_send()

    @pl.when(across)
    def _():
        share_core().wait_send()

    for n in range(2):
        part_sends(n, lambda copy: copy.wait_send())
        for level in range(3):
            level_copies(n, level, lambda copy: copy.wait_send())

        @pl.when(core == 0)
        def _(n=n):
            core_copy(n).wait_send()

    out.wait()


def exchange(maps, live, parent, updates):
    hbm = pl.BlockSpec(memory_space=pl.ANY)
    smem = pl.BlockSpec(memory_space=pltpu.SMEM)
    f32 = jnp.float32
    return pl.pallas_call(
        exchange_body,
        out_shape=(
            jax.ShapeDtypeStruct((8, 4, 256, 512), f32),
            jax.ShapeDtypeStruct((4, 256, 2048), f32),
            jax.ShapeDtypeStruct((512, 1024), f32),
        ),
        in_specs=[smem, smem, hbm, hbm],
        out_specs=(hbm, hbm, hbm),
        scratch_shapes=[
            pltpu.VMEM((4, 256, 256), f32),
            pltpu.VMEM((4, 256, 256), f32),
            pltpu.VMEM((256, 512), f32),
            pltpu.VMEM((4, 256, 512), f32),
            pltpu.VMEM((1024, 1024), f32),
            pltpu.VMEM((512, 512), f32),
            pltpu.VMEM((128, 128), f32),
            pltpu.VMEM((512, 1024), f32),
            *[pltpu.VMEM((64, 8, width), f32) for width in WIDTHS],
            pltpu.SemaphoreType.DMA((SLOTS,)),
            pltpu.SemaphoreType.DMA((SLOTS,)),
            pltpu.SemaphoreType.DMA((3,)),
            pltpu.SemaphoreType.DMA((2, 64)),
            pltpu.SemaphoreType.DMA((2,)),
        ],
        compiler_params=pltpu.CompilerParams(has_side_effects=True, vmem_limit_bytes=40 * 2**20),
    )(maps, live, parent, updates)


def per_device(parent, updates, maps, live):
    panel, bulk, wt = exchange(maps, live, parent, updates)
    place = jnp.stack([lax.axis_index("child"), lax.axis_index("col")]).astype(jnp.int32)
    return finish(place, maps, live, parent, bulk, panel.reshape(8, 1024, 512), wt)


def solution(mesh):
    in_specs = (P("child", "col"), P("child", "col", None), P(), P())
    return jax.shard_map(
        per_device, mesh=mesh, in_specs=in_specs, out_specs=P("child", "col"), check_vma=False
    )
```

```python
import functools

import jax
import jax.numpy as jnp
from jax import lax
from jax.experimental import pallas as pl
from jax.experimental.pallas import tpu as pltpu
from jax.sharding import PartitionSpec as P

HIGHEST = lax.Precision.HIGHEST


def recip(d):
    r = pl.reciprocal(d, approx=True)
    return r*(2.0-d*r)
def rsq(d):
    r = lax.rsqrt(d)
    return r*(1.5-0.5*d*r*r)
def diag_inverse(tile):
    rows=[tile[8*g:8*g+8,:] for g in range(16)]
    lane=lax.broadcasted_iota(jnp.int32,(8,128),1)
    sub=lax.broadcasted_iota(jnp.int32,(8,128),0)
    wide=lambda v: jnp.broadcast_to(v,(8,128))
    for m in range(16):
        o=8*m
        V=rows[m]
        inside=(lane>=o)&(lane<o+8)
        b={(i,q): wide(V[i:i+1,o+q:o+q+1]) for i in range(8) for q in range(i+1)}
        cols={(g,q): wide(rows[g][:,o+q:o+q+1]) for g in range(m+1,16) for q in range(8)}
        V=jnp.where(inside, jnp.where(lane-o==sub,1.0,0.0), V)
        v=[wide(V[i:i+1,:]) for i in range(8)]
        if m<15:
            after=jnp.where(inside,0.0,rows[m+1])
            ce=[cols[m+1,q] for q in range(8)]
        l={}; rd=[]
        for q in range(8):
            rd.append(recip(b[q,q]))
            for i in range(q+1,8):
                for c in range(q+1,i+1):
                    b[i,c]=b[i,c]-(b[i,q]*b[c,q])*rd[q]
                l[i,q]=b[i,q]*rd[q]
                v[i]=v[i]-l[i,q]*v[q]
            if m<15:
                times=ce[q]*rd[q]
                after=after-times*v[q]
                for c in range(q+1,8):
                    ce[c]=ce[c]-times*b[c,q]
        if m<15:
            rows[m+1]=after
        new=v[0]*rsq(b[0,0])
        for i in range(1,8):
            new=jnp.where(sub==i, v[i]*rsq(b[i,i]), new)
        rows[m]=new
        if m<14:
            t=[v[i]*rd[i] for i in range(8)]
            for i in range(6,-1,-1):
                for c in range(i+1,8):
                    t[i]=t[i]-l[c,i]*t[c]
            for g in range(m+2,16):
                acc=jnp.where(inside,0.0,rows[g])
                for q in range(8):
                    acc=acc-cols[g,q]*t[q]
                rows[g]=acc
    full=jnp.concatenate(rows,0)
    r=lax.broadcasted_iota(jnp.int32,(128,128),0); c=lax.broadcasted_iota(jnp.int32,(128,128),1)
    return jnp.where(c<=r, full, 0.0)
def block_at(k):
    return pl.ds(pl.multiple_of(k*128,128),128)
def factor_start(S,inv):
    inv[...]=diag_inverse(S[0:128,0:128])
def factor_step(S,inv,k):
    at=block_at(k)
    r=lax.broadcasted_iota(jnp.int32,(128,128),0); c=lax.broadcasted_iota(jnp.int32,(128,128),1)
    S[at,at]=jnp.where(r==c,1.0,0.0)
    row=jnp.dot(inv[...],S[at,:],precision=HIGHEST,preferred_element_type=jnp.float32)
    S[at,:]=row
    def clear(i,_):
        S[block_at(i),at]=jnp.zeros((128,128),jnp.float32)
        return 0
    lax.fori_loop(k+1,8,clear,0)
    @pl.when(k<7)
    def _():
        nx=block_at(k+1)
        tn=lambda a,b: lax.dot_general(a,b,(((0,),(0,)),((),())),precision=HIGHEST,preferred_element_type=jnp.float32)
        S[nx,:]=S[nx,:]-tn(S[at,nx],S[at,:])
        tile=S[nx,nx]
        cols=lax.broadcasted_iota(jnp.int32,(128,1024),1)
        full=S[at,:]
        left=jnp.where(cols>=(k+2)*128,full,0.0)
        inv[...]=diag_inverse(tile)
        for g in range(2,8):
            S[g*128:g*128+128,:]=S[g*128:g*128+128,:]-tn(left[:,g*128:g*128+128],full)


def finish_body(place_ref, map_ref, live_ref, parent_ref, upd_ref, panel_ref, wt_ref, out_ref, whi, wlo, acc):
    i=pl.program_id(0)
    r=place_ref[0]; j=place_ref[1]
    @pl.when(i==0)
    def _():
        w=wt_ref[...]
        h=w.astype(jnp.bfloat16)
        whi[...]=h
        wlo[...]=(w-h.astype(jnp.float32)).astype(jnp.bfloat16)
    keep=jnp.where(j>=2,1.0,0.0).astype(jnp.float32)
    acc[...]=jnp.zeros((512,512),jnp.float32)
    for c in range(4):
        for q in range(2):
            col=2*j+q
            bq=map_ref[c,col]-4*j
            lq=live_ref[c,col].astype(jnp.float32)*keep
            for p in range(2):
                row=16*r+2*i+p
                ap=map_ref[c,row]-4*(8*r+i)
                w=lq*live_ref[c,row].astype(jnp.float32)
                dst=(pl.ds(pl.multiple_of(bq*128,128),128),pl.ds(pl.multiple_of(ap*128,128),128))
                acc[dst]=acc[dst]+w*upd_ref[c,q*128:q*128+128,p*128:p*128+128]
    dot=lambda x,y: jnp.dot(x,y,preferred_element_type=jnp.float32)
    for h in range(0,512,512):
        a=panel_ref[0,:,h:h+512]
        ahi=a.astype(jnp.bfloat16)
        alo=(a-ahi.astype(jnp.float32)).astype(jnp.bfloat16)
        product=dot(whi[...],ahi)+(dot(whi[...],alo)+dot(wlo[...],ahi))
        total=(product+acc[:,h:h+512]).T+keep*parent_ref[h:h+512,:]
        g=r*4096+i*512+h+lax.broadcasted_iota(jnp.int32,(512,512),0)
        s=j*512+lax.broadcasted_iota(jnp.int32,(512,512),1)
        out_ref[h:h+512,:]=jnp.where(g<jnp.minimum(s,1024),0.0,total)
def finish(place,maps,live,parent,upd,panel,wt):
    spec=pltpu.PrefetchScalarGridSpec(num_scalar_prefetch=3,grid=(8,),
      in_specs=[pl.BlockSpec((512,512),lambda i,*_:(i,0)),
                pl.BlockSpec((4,256,256),lambda i,*_:(0,0,i)),
                pl.BlockSpec((1,1024,512),lambda i,*_:(i,0,0)),
                pl.BlockSpec((512,1024),lambda i,*_:(0,0))],
      out_specs=pl.BlockSpec((512,512),lambda i,*_:(i,0)),
      scratch_shapes=[pltpu.VMEM((512,1024),jnp.bfloat16),pltpu.VMEM((512,1024),jnp.bfloat16),pltpu.VMEM((512,512),jnp.float32)])
    return pl.pallas_call(finish_body,grid_spec=spec,out_shape=jax.ShapeDtypeStruct((4096,512),jnp.float32),
      compiler_params=pltpu.CompilerParams(vmem_limit_bytes=48*2**20),
      cost_estimate=pl.CostEstimate(flops=3*2*4096*512*1024,bytes_accessed=45*2**20,transcendentals=0))(place,maps,live,parent,upd,panel,wt)


MESH = pl.DeviceIdType.MESH


class Links:
    def __init__(self, send_sem, recv_sem):
        self.send_sem, self.recv_sem, self.used = send_sem, recv_sem, 0
        self.pending = []

    def slot(self):
        self.used += 1
        return self.used - 1

    def slots(self, count):
        self.used += count
        return self.used - count

    def copy(self, slot, source, target, device):
        return pltpu.make_async_remote_copy(
            src_ref=source,
            dst_ref=target,
            send_sem=self.send_sem.at[slot],
            recv_sem=self.recv_sem.at[slot],
            device_id=device,
            device_id_type=MESH,
        )

    def send(self, slot, ends):
        self.copy(slot, *ends()).start()
        self.pending.append((slot, ends))

    def landed(self, slot, region, device):
        self.copy(slot, region, region, device).wait_recv()

    def drain(self):
        for slot, ends in self.pending:
            self.copy(slot, *ends()).wait_send()
        self.pending = []


SLOTS = 128
BULK = (0, 2, 1, 2, 1, 2)
WIDTHS = (768, 512)
WHERE = ((0, 0), (0, 128), (0, 384), (1, 0))


def exchange_body(
    map_ref, live_ref, parent_ref, upd_ref, panel_ref, bulk_ref, wt_ref,
    raw, turned, chunk, top, square, corner, inverse, weight, set_0, set_1,
    send_sem, recv_sem, local_sem, part_send, part_recv,
):
    r = lax.axis_index("child")
    j = lax.axis_index("col")
    y, x, zl = j // 8, (j // 2) % 4, j % 2
    t = j % 8
    zh = r // 2
    core = r % 2
    links = Links(send_sem, recv_sem)
    is_root = (r == 0) & (j == 0)
    source_col = 8 * r + t

    def col_at(ny, nx, nz):
        return ny * 8 + nx * 2 + nz

    def x_dev(step):
        return (r, col_at(y, (x + step) % 4, zl))

    def y_dev(step):
        return (r, col_at((y + step) % 4, x, zl))

    def panel_part(piece, ny):
        return panel_ref.at[piece, ny]

    head_slot = links.slots(4)
    strip_slot = links.slots(16)

    def strip(n):
        return upd_ref.at[0, :, pl.ds(256 * (n // 2), 256)]

    def head_copy(n):
        return links.copy(head_slot + n, parent_ref.at[pl.ds(256 * n, 256), :], chunk, (y, n * 8 + t))

    def strip_copy(n):
        return links.copy(strip_slot + 4 * r + n, strip(n), raw.at[r], (y, n * 8 + t))

    def panel_sends(act):
        for n in range(4):
            @pl.when((r != y) | (y != n))
            def _(n=n):
                act(strip_copy(n))

            @pl.when((r == 0) & (y + n > 0))
            def _(n=n):
                act(head_copy(n))

    panel_sends(lambda copy: copy.start())
    own_head = pltpu.make_async_copy(parent_ref.at[pl.ds(0, 256), :], chunk, local_sem.at[1])

    def own_strip():
        part = upd_ref.at[0, :, pl.ds(pl.multiple_of(256 * (y // 2), 256), 256)]
        return pltpu.make_async_copy(part, raw.at[r], local_sem.at[2])

    @pl.when((r == 0) & (y == 0))
    def _():
        own_head.start()

    @pl.when(r == y)
    def _():
        own_strip().start()

    partners = [r + 1 - 2 * core, (r + 2) % 4, 3 - r]
    bulk_slot = links.slot()
    bulk_queue = [(n, m, links.slot()) for m in range(4) for n in (1, 2)]
    bulk_all = list(bulk_queue)

    def bulk_send():
        def ends():
            rows = pl.ds(pl.multiple_of(partners[0] * 2048, 2048), 2048)
            return upd_ref.at[0, :, rows], bulk_ref.at[r], (partners[0], j)

        links.send(bulk_slot, ends)

    def bulk_some(count):
        for _ in range(count):
            n, m, slot = bulk_queue.pop(0)

            def ends(n=n, m=m):
                rows = pl.ds(pl.multiple_of(partners[n] * 2048 + 512 * m, 512), 512)
                return upd_ref.at[0, :, rows], bulk_ref.at[r, :, pl.ds(512 * m, 512)], (partners[n], j)

            links.send(slot, ends)

    own_rows = pl.ds(pl.multiple_of(r * 2048, 2048), 2048)
    own_bulk = pltpu.make_async_copy(upd_ref.at[0, :, own_rows], bulk_ref.at[r], local_sem.at[0])
    bulk_some(BULK[0])
    weight[...] = jnp.zeros((512, 1024), jnp.float32)

    @pl.when(r == y)
    def _():
        own_strip().wait()

    for c in range(4):
        @pl.when((r != c) | (r != y))
        def _(c=c):
            links.landed(strip_slot + 4 * c + y, raw.at[c], (c, source_col))
        for q in range(2):
            for p in range(2):
                turned[c, p * 128:(p + 1) * 128, q * 128:(q + 1) * 128] = raw[
                    c, q * 128:(q + 1) * 128, p * 128:(p + 1) * 128
                ].T

    @pl.when((r == 0) & (y == 0))
    def _():
        own_head.wait()

    @pl.when((r > 0) | (y > 0))
    def _():
        links.landed(head_slot + y, chunk, (0, source_col))

    def place(step, _):
        a, b = step // 4, step % 4
        rows = pl.ds(pl.multiple_of(a * 128, 128), 128)
        cols = pl.ds(pl.multiple_of(b * 128, 128), 128)
        total = chunk[rows, cols]
        for c in range(4):
            for p in range(2):
                row = 2 * (y // 2) + p
                row_weight = jnp.where(map_ref[c, row] == 2 * y + a, live_ref[c, row], 0)
                for q in range(2):
                    col = 2 * source_col + q
                    col_weight = jnp.where(map_ref[c, col] == 4 * source_col + b, live_ref[c, col], 0)
                    both = (row_weight * col_weight).astype(jnp.float32)
                    total = total + both * turned[c, p * 128:(p + 1) * 128, q * 128:(q + 1) * 128]
        chunk[rows, cols] = total
        return 0

    lax.fori_loop(0, 8, place, 0)

    pivot_slot = links.slots(8)

    def pivot_part(side, n):
        if side == 0:
            return square.at[pl.ds(pl.multiple_of(n * 256, 256), 256), pl.ds(0, 512)]
        return corner.at[pl.ds(pl.multiple_of(n * 256 - 512, 256), 256), :]

    def pivot_sends(act):
        for side in range(2):
            @pl.when((r == 0) & (t == side) & (y > side))
            def _(side=side):
                act(links.copy(pivot_slot + 4 * side + y, chunk, pivot_part(side, y), (0, 0)))

    pivot_sends(lambda copy: copy.start())
    pair_slot = links.slot()
    links.send(pair_slot, lambda: (chunk, panel_part(t, y), (r, j + 1 - 2 * zl)))
    own_chunk = pltpu.make_async_copy(chunk, panel_part(t, y), local_sem.at[1])
    own_chunk.start()
    bulk_send()
    own_bulk.start()

    def root_square():
        square[0:256, 0:512] = chunk[...]
        square[512:1024, 512:1024] = jnp.zeros((512, 512), jnp.float32)
        for n in range(1, 4):
            links.landed(pivot_slot + n, pivot_part(0, n), (0, 8 * n))
        for a in range(4):
            for b in range(4):
                square[a * 128:(a + 1) * 128, 512 + b * 128:640 + b * 128] = square[
                    512 + b * 128:640 + b * 128, a * 128:(a + 1) * 128
                ].T
        factor_start(square, inverse)

    def root_corner():
        for n in range(2, 4):
            links.landed(pivot_slot + 4 + n, pivot_part(1, n), (0, 8 * n + 1))
        square[512:1024, 512:1024] = square[512:1024, 512:1024] + corner[...]

    OFFSETS = (0, 3, 1, 2)

    def pass_on(slot, region, device):
        def ends():
            here_and_there = region()
            return here_and_there, here_and_there, device()

        links.send(slot, ends)

    def item(kind, nx, ny):
        return panel_ref.at[pl.ds(2 * nx, 2), ny, pl.ds(kind * 128, 128), :]

    def half(kind, nx, ny, h):
        return panel_ref.at[2 * nx + h, ny, pl.ds(kind * 128, 128), :]

    def spot(kind, along, across):
        if kind == 0:
            return (x + along) % 4, (y + across) % 4
        return (x + across) % 4, (y + along) % 4

    def first_dev(kind, step):
        return x_dev(step) if kind == 0 else y_dev(step)

    def second_dev(kind, step):
        return y_dev(step) if kind == 0 else x_dev(step)

    one = [[links.slot() for _ in range(4)] for _ in range(2)]
    two = [{o: [links.slot() for _ in range(4)] for o in OFFSETS} for _ in range(2)]

    def second_send(o):
        for kind in range(2):
            region = lambda kind=kind: item(kind, *spot(kind, o, 0))
            pass_on(two[kind][o][0], region, functools.partial(second_dev, kind, 1))
            pass_on(two[kind][o][1], region, functools.partial(second_dev, kind, 3))

    def second_forward(o):
        for kind in range(2):
            links.landed(two[kind][o][0], item(kind, *spot(kind, o, 3)), second_dev(kind, 3))
            region = lambda kind=kind: half(kind, *spot(kind, o, 3), 0)
            pass_on(two[kind][o][2], region, functools.partial(second_dev, kind, 1))
            links.landed(two[kind][o][1], item(kind, *spot(kind, o, 1)), second_dev(kind, 1))
            region = lambda kind=kind: half(kind, *spot(kind, o, 1), 1)
            pass_on(two[kind][o][3], region, functools.partial(second_dev, kind, 3))

    def second_end(o):
        for kind in range(2):
            links.landed(two[kind][o][2], half(kind, *spot(kind, o, 2), 0), second_dev(kind, 3))
            links.landed(two[kind][o][3], half(kind, *spot(kind, o, 2), 1), second_dev(kind, 1))

    def event_pair():
        own_chunk.wait()
        links.landed(pair_slot, panel_part(t + 1 - 2 * zl, y), (r, j + 1 - 2 * zl))
        for kind in range(2):
            region = functools.partial(item, kind, x, y)
            pass_on(one[kind][0], region, functools.partial(first_dev, kind, 1))
            pass_on(one[kind][1], region, functools.partial(first_dev, kind, 3))
        second_send(0)
        bulk_some(BULK[1])

    def event_near():
        for kind in range(2):
            links.landed(one[kind][0], item(kind, *spot(kind, 3, 0)), first_dev(kind, 3))
            region = lambda kind=kind: half(kind, *spot(kind, 3, 0), 0)
            pass_on(one[kind][2], region, functools.partial(first_dev, kind, 1))
            links.landed(one[kind][1], item(kind, *spot(kind, 1, 0)), first_dev(kind, 1))
            region = lambda kind=kind: half(kind, *spot(kind, 1, 0), 1)
            pass_on(one[kind][3], region, functools.partial(first_dev, kind, 3))
        second_send(3)
        second_send(1)

    def event_far():
        for kind in range(2):
            links.landed(one[kind][2], half(kind, *spot(kind, 2, 0), 0), first_dev(kind, 3))
            links.landed(one[kind][3], half(kind, *spot(kind, 2, 0), 1), first_dev(kind, 1))
        second_send(2)

    home = r == y
    across = r == (y + 2) % 4
    home_core = r == y + 1 - 2 * (y % 2)
    share_slots = [links.slot() for _ in range(3)]

    def own_top():
        return pltpu.make_async_copy(panel_ref.at[t], top, local_sem.at[2])

    def share_copies():
        return (
            links.copy(share_slots[0], panel_ref.at[t], top, ((r + 2) % 4, j)),
            links.copy(share_slots[1], panel_ref.at[t], top, (r + 1 - 2 * core, j)),
        )

    def share_core():
        return links.copy(share_slots[2], top, top, (r + 1 - 2 * core, j))

    def event_share():
        second_end(0)

        @pl.when(home)
        def _():
            for copy in share_copies():
                copy.start()
            own_top().start()

    def event_share_across():
        @pl.when(home)
        def _():
            own_top().wait()

        @pl.when(home_core)
        def _():
            links.landed(share_slots[1], top, (y, j))

        @pl.when(across)
        def _():
            links.landed(share_slots[0], top, (y, j))
            share_core().start()

    def event_share_end():
        @pl.when(jnp.logical_not(home | home_core | across))
        def _():
            links.landed(share_slots[2], top, ((y + 2) % 4, j))

    z = zh * 2 + zl
    part = y * 16 + x * 4 + z
    sets = (set_0, set_1)
    ring = [[links.slot() for _ in range(9)] for _ in range(2)]
    core_slots = [links.slot() for _ in range(2)]

    def chip(ny, nx, nz):
        return (2 * (nz // 2), col_at(ny, nx, nz % 2))

    def part_copy(n, s, device):
        piece = sets[n].at[pl.ds(s, 1)]
        return pltpu.make_async_remote_copy(
            src_ref=piece, dst_ref=piece, send_sem=part_send.at[n, s], recv_sem=part_recv.at[n],
            device_id=device, device_id_type=MESH,
        )

    def part_sends(n, act):
        @pl.when(is_root)
        def _():
            def go(s, _):
                act(part_copy(n, s, chip(s // 16, (s // 4) % 4, s % 4)))
                return 0

            lax.fori_loop(1, 64, go, 0)

    def span(n, level, nz, nx, ny):
        if level == 0:
            return sets[n].at[pl.ds(ny * 16 + nx * 4 + nz, 1)]
        if level == 1:
            return sets[n].at[pl.ds(ny * 16 + nx * 4, 4)]
        return sets[n].at[pl.ds(ny * 16, 16)]

    def moved(level, step):
        if level == 0:
            return (z + step) % 4, x, y
        if level == 1:
            return z, (x + step) % 4, y
        return z, x, (y + step) % 4

    def level_copies(n, level, act):
        for step in range(1, 4):
            nz, nx, ny = moved(level, step)

            @pl.when((core == 0) & (nz + nx + ny > 0))
            def _(step=step, nz=nz, nx=nx, ny=ny):
                region = span(n, level, z, x, y)
                act(links.copy(ring[n][level * 3 + step - 1], region, region, chip(ny, nx, nz)))

    def level_end(n, level):
        @pl.when((core == 0) & (part > 0))
        def _():
            for step in range(1, 4):
                nz, nx, ny = moved(level, 4 - step)
                links.landed(ring[n][level * 3 + step - 1], span(n, level, nz, nx, ny), chip(ny, nx, nz))

    def core_copy(n):
        return links.copy(core_slots[n], sets[n], sets[n], (r + 1, j))

    def keep(n):
        half = 128 * (n + 1)
        which, at = WHERE[n]
        rows = n * 256 + lax.broadcasted_iota(jnp.int32, (256, half), 0)
        cols = lax.broadcasted_iota(jnp.int32, (256, half), 1)
        for h in range(2):
            kept = square[n * 256:(n + 1) * 256, h * half:(h + 1) * half]
            kept = jnp.where(cols + h * half <= rows, kept, 0.0)
            sets[which][h * 32:(h + 1) * 32, :, at:at + half] = kept.reshape(32, 8, half)

    def leave(n):
        @pl.when(is_root)
        def _():
            for m in ((0, 1, 2), (3,))[n]:
                keep(m)

        part_sends(n, lambda copy: copy.start())

    def over_z(n):
        @pl.when((core == 0) & (part > 0))
        def _():
            part_copy(n, part, (0, 0)).wait_recv()

        level_copies(n, 0, lambda copy: copy.start())

    def over_x(n):
        level_end(n, 0)
        level_copies(n, 1, lambda copy: copy.start())

    def over_y(n):
        level_end(n, 1)
        level_copies(n, 2, lambda copy: copy.start())

    def over_core(n):
        level_end(n, 2)

        @pl.when(core == 0)
        def _():
            core_copy(n).start()

    def split(a):
        high = a.astype(jnp.bfloat16)
        return high, (a - high.astype(jnp.float32)).astype(jnp.bfloat16)

    def times(a, b, dims):
        dot = lambda u, v: lax.dot_general(u, v, (dims, ((), ())), preferred_element_type=jnp.float32)
        return dot(a[0], b[0]) + (dot(a[0], b[1]) + dot(a[1], b[0]))

    def weigh(n):
        half = 128 * (n + 1)
        which, at = WHERE[n]
        width = 2 * half

        def lower():
            return jnp.concatenate(
                [sets[which][h * 32:(h + 1) * 32, :, at:at + half].reshape(256, half) for h in range(2)], axis=1
            )

        @pl.when(j == n // 2)
        def _():
            weight[n % 2 * 256:(n % 2 + 1) * 256, 0:width] = lower()

        @pl.when(j >= 2)
        def _():
            part_of = split(lower())
            solved = times(part_of, split(top[0:n + 1].reshape(width, 512)), ((1,), (0,)))
            weight[:, 0:width] = weight[:, 0:width] - times(split(solved), part_of, ((0,), (0,)))

    def arrive(n):
        @pl.when(core == 1)
        def _():
            links.landed(core_slots[n], sets[n], (r - 1, j))

        for m in ((0, 1, 2), (3,))[n]:
            weigh(m)

    do = functools.partial
    plan = {
        0: [event_far],
        1: [do(second_forward, 0), do(bulk_some, BULK[3])],
        3: [do(second_forward, 3)],
        4: [event_share],
        5: [do(leave, 0), do(second_forward, 1), do(over_z, 0), do(bulk_some, BULK[4])],
        6: [do(over_x, 0)],
        7: [do(leave, 1), do(over_y, 0), do(over_z, 1), do(second_forward, 2), do(over_x, 1)],
    }

    def step(k, _):
        @pl.when(is_root & (k == 3))
        def _():
            root_corner()

        @pl.when(is_root)
        def _():
            factor_step(square, inverse, k)

        for n, events in plan.items():
            @pl.when(k == n)
            def _(events=events):
                for event in events:
                    event()

        return 0

    event_pair()
    event_near()

    @pl.when(is_root)
    def _():
        root_square()

    bulk_some(BULK[2])
    lax.fori_loop(0, 8, step, 0)
    event_share_across()
    bulk_some(BULK[5])
    over_core(0)
    over_y(1)
    event_share_end()
    arrive(0)
    over_core(1)
    arrive(1)
    out = pltpu.make_async_copy(weight, wt_ref, local_sem.at[1])
    out.start()
    for o in OFFSETS[1:]:
        second_end(o)
    own_bulk.wait()
    links.landed(bulk_slot, bulk_ref.at[partners[0]], (partners[0], j))
    for n, m, slot in bulk_all:
        links.landed(slot, bulk_ref.at[partners[n], :, pl.ds(512 * m, 512)], (partners[n], j))
    links.drain()
    panel_sends(lambda copy: copy.wait_send())
    pivot_sends(lambda copy: copy.wait_send())

    @pl.when(home)
    def _():
        for copy in share_copies():
            copy.wait_send()

    @pl.when(across)
    def _():
        share_core().wait_send()

    for n in range(2):
        part_sends(n, lambda copy: copy.wait_send())
        for level in range(3):
            level_copies(n, level, lambda copy: copy.wait_send())

        @pl.when(core == 0)
        def _(n=n):
            core_copy(n).wait_send()

    out.wait()


def exchange(maps, live, parent, updates):
    hbm = pl.BlockSpec(memory_space=pl.ANY)
    smem = pl.BlockSpec(memory_space=pltpu.SMEM)
    f32 = jnp.float32
    return pl.pallas_call(
        exchange_body,
        out_shape=(
            jax.ShapeDtypeStruct((8, 4, 256, 512), f32),
            jax.ShapeDtypeStruct((4, 256, 2048), f32),
            jax.ShapeDtypeStruct((512, 1024), f32),
        ),
        in_specs=[smem, smem, hbm, hbm],
        out_specs=(hbm, hbm, hbm),
        scratch_shapes=[
            pltpu.VMEM((4, 256, 256), f32),
            pltpu.VMEM((4, 256, 256), f32),
            pltpu.VMEM((256, 512), f32),
            pltpu.VMEM((4, 256, 512), f32),
            pltpu.VMEM((1024, 1024), f32),
            pltpu.VMEM((512, 512), f32),
            pltpu.VMEM((128, 128), f32),
            pltpu.VMEM((512, 1024), f32),
            *[pltpu.VMEM((64, 8, width), f32) for width in WIDTHS],
            pltpu.SemaphoreType.DMA((SLOTS,)),
            pltpu.SemaphoreType.DMA((SLOTS,)),
            pltpu.SemaphoreType.DMA((3,)),
            pltpu.SemaphoreType.DMA((2, 64)),
            pltpu.SemaphoreType.DMA((2,)),
        ],
        compiler_params=pltpu.CompilerParams(has_side_effects=True, vmem_limit_bytes=40 * 2**20),
    )(maps, live, parent, updates)


def per_device(parent, updates, maps, live):
    panel, bulk, wt = exchange(maps, live, parent, updates)
    place = jnp.stack([lax.axis_index("child"), lax.axis_index("col")]).astype(jnp.int32)
    return finish(place, maps, live, parent, bulk, panel.reshape(8, 1024, 512), wt)


def solution(mesh):
    in_specs = (P("child", "col"), P("child", "col", None), P(), P())
    return jax.shard_map(
        per_device, mesh=mesh, in_specs=in_specs, out_specs=P("child", "col"), check_vma=False
    )
```
